512 devices in a mesh: row: 32 (over x, y, core), col: 16 (over z).
Axes of the slice: x: 4, y: 4, z: 16, core: 2. Of those that a mesh axis runs over, the one named last changes fastest.
Arguments:
- slip_rate: bfloat16 [128, 32, 128, 256], P('row', 'col'), may hold values from -6 to 6
- near_lists: int32 [128, 32, 6], P('row', 'col'), may hold values from 0 to 8, as said below
- near_blocks: bfloat16 [128, 32, 6, 128, 128], P('row', 'col'), may hold values from -0.21875 to 0.21875
- source_basis: bfloat16 [128, 32, 64, 128], P('row', 'col'), may hold values from -0.5 to 0.5
- target_basis: bfloat16 [128, 32, 64, 128], P('row', 'col'), may hold values from -0.75 to 0.75
- leaf_up: float32 [128, 32, 64, 64], P('row', 'col'), may hold values from -0.25 to 0.25
- leaf_down: float32 [128, 32, 64, 64], P('row', 'col'), may hold values from -0.75 to 0.75
- strip_up: float32 [32, 4, 2, 64, 64], P('row'), may hold values from -0.5 to 0.5
- strip_down: float32 [32, 4, 2, 64, 64], P('row'), may hold values from -0.75 to 0.75
- strip_lists: int32 [32, 16], P('row'), may hold values from 0 to 31, as said below
- coupling: float32 [32, 16, 64, 64], P('row'), may hold values from -0.1875 to 0.1875
Outputs:
- stress_rate: bfloat16 [128, 32, 128, 256], P('row', 'col')
The draws below stay inside these ranges and needn't reach their ends.
Inputs may be any that keep to these rules, and one draw needn't show every extreme that they name: `near_lists`: entry q names the neighbour leaf at offset (q // 3 - 1, q % 3 - 1); the first entry of every leaf is 4, its own block; the 6 entries of one leaf are distinct. `strip_lists`: strip r lists 16 distinct strips s with |s - r| >= 2.
All inputs are finite; a program needn't handle non-finite values.
Results may differ from the reference program's by a relative error of at most 0.0047.
Values may be sent and summed in bfloat16 or wider, within the bound.
No kernel may reach another device: no remote copies, remote signals or barrier semaphores. Data moves between devices by JAX's collectives and lax.ppermute only.
A program may use at most 64 MiB of HBM per device.

```python
import jax
import jax.numpy as jnp
from jax import lax

LEAF = 128
RANK = 64
MEMBERS = 256
NEAR = 6
ALONG = 4
DIP = 2
CLEV = 4
FAR_STRIPS = 16
STRIKE_LEAVES = 128
DIP_LEAVES = 32
N_ROW = 32
N_COL = 16


def draw_near_lists(key, part):
    key = jax.random.fold_in(key, 5)
    slot_index = jnp.arange(8, dtype=jnp.int32)[None, None, :]
    ranking = jax.random.randint(key, (STRIKE_LEAVES, DIP_LEAVES, 8), 0, 1048576, dtype=jnp.int32) * 8 + slot_index
    picked = lax.top_k(ranking, NEAR - 1)[1].astype(jnp.int32)
    others = picked + (picked >= 4).astype(jnp.int32)
    own_block = jnp.full((STRIKE_LEAVES, DIP_LEAVES, 1), 4, dtype=jnp.int32)
    return jnp.concatenate([own_block, others], axis=2)


def draw_strip_lists(key, part):
    key = jax.random.fold_in(key, 11)
    target_strip = jnp.arange(N_ROW, dtype=jnp.int32)[:, None]
    source_strip = jnp.arange(N_ROW, dtype=jnp.int32)[None, :]
    ranking = jax.random.randint(key, (N_ROW, N_ROW), 0, 1048576, dtype=jnp.int32) * N_ROW + source_strip
    corner_pair = (target_strip == 0) & (source_strip == N_ROW - 1) | (target_strip == N_ROW - 1) & (source_strip == 0)
    ranking = jnp.where(corner_pair, ranking + 67108864, ranking)
    ranking = jnp.where(jnp.abs(target_strip - source_strip) <= 1, -1 - source_strip, ranking)
    return lax.top_k(ranking, FAR_STRIPS)[1].astype(jnp.int32)


def level_of(rng, shape, cuts, least, largest):
    level, own = 1.0, jax.random.fold_in(rng, 6)
    for axis_at, blocks in cuts:
        heights = jnp.exp(jax.random.uniform(jax.random.fold_in(own, axis_at), (blocks,), jnp.float32, least / len(cuts), largest / len(cuts)))
        level = level * jnp.repeat(heights, shape[axis_at] // blocks).reshape([-1 if axis == axis_at else 1 for axis in range(len(shape))])
    return level


def bell_draw(stream_key, dims, width, reach, split=(), kind=jnp.bfloat16):
    drawn = width * jax.random.normal(stream_key, dims, jnp.float32)
    if split:
        drawn = drawn * level_of(stream_key, dims, split, -0.22, 0.18)
    return jnp.clip(drawn, -reach, reach).astype(kind)


def setup_inputs(seed: int = 0) -> dict:
    key_of = jax.random.split(jax.random.key(seed), 12)
    slip_rate = bell_draw(key_of[0], (STRIKE_LEAVES, DIP_LEAVES, LEAF, MEMBERS), 1.0, 6.0, ((0, 32), (1, 16)))
    near_lists = draw_near_lists(jax.random.fold_in(key_of[11], 71), 0)
    near_blocks = bell_draw(key_of[2], (STRIKE_LEAVES, DIP_LEAVES, NEAR, LEAF, LEAF), (LEAF * NEAR) ** -0.5, 0.21875, ((0, 32), (1, 16)))
    source_basis = bell_draw(key_of[3], (STRIKE_LEAVES, DIP_LEAVES, RANK, LEAF), LEAF ** -0.5, 0.5, ((0, 32), (1, 16)))
    target_basis = bell_draw(key_of[4], (STRIKE_LEAVES, DIP_LEAVES, RANK, LEAF), RANK ** -0.5, 0.75, ((0, 32), (1, 16)))
    leaf_up = bell_draw(key_of[5], (STRIKE_LEAVES, DIP_LEAVES, RANK, RANK), (RANK * ALONG * DIP) ** -0.5, 0.25, ((0, 32), (1, 16)), jnp.float32)
    leaf_down = bell_draw(key_of[6], (STRIKE_LEAVES, DIP_LEAVES, RANK, RANK), RANK ** -0.5, 0.75, ((0, 32), (1, 16)), jnp.float32)
    strip_up = bell_draw(key_of[7], (N_ROW, CLEV, 2, RANK, RANK), (2 * RANK) ** -0.5, 0.5, ((0, 32),), jnp.float32)
    strip_down = bell_draw(key_of[8], (N_ROW, CLEV, 2, RANK, RANK), RANK ** -0.5, 0.75, ((0, 32),), jnp.float32)
    strip_lists = draw_strip_lists(jax.random.fold_in(key_of[11], 71), 0)
    coupling = bell_draw(key_of[10], (N_ROW, FAR_STRIPS, RANK, RANK), (RANK * FAR_STRIPS) ** -0.5, 0.1875, ((0, 32),), jnp.float32)
    return dict(slip_rate=slip_rate, near_lists=near_lists, near_blocks=near_blocks, source_basis=source_basis, target_basis=target_basis, leaf_up=leaf_up, leaf_down=leaf_down, strip_up=strip_up, strip_down=strip_down, strip_lists=strip_lists, coupling=coupling)


def reference(slip_rate, near_lists, near_blocks, source_basis, target_basis, leaf_up, leaf_down, strip_up, strip_down, strip_lists, coupling):
    highest = lax.Precision.HIGHEST
    strike_count = slip_rate.shape[0]
    dip_count = slip_rate.shape[1]
    rank_width = source_basis.shape[2]
    member_count = slip_rate.shape[3]
    padded = jnp.pad(slip_rate, ((1, 1), (1, 1), (0, 0), (0, 0)))

    def near_row(strip_row):
        rows = lax.dynamic_slice_in_dim(padded, strip_row.astype(jnp.int32), 3, 0)
        views = jnp.stack([rows[row_off, col_off:col_off + dip_count] for row_off in range(3) for col_off in range(3)], axis=1)
        leaf_lists = lax.dynamic_index_in_dim(near_lists, strip_row.astype(jnp.int32), 0, keepdims=False)
        chosen = jnp.take_along_axis(views, leaf_lists[:, :, None, None], axis=1)
        blocks = lax.dynamic_index_in_dim(near_blocks, strip_row.astype(jnp.int32), 0, keepdims=False)
        return jnp.einsum("bnij,bnje->bie", blocks.astype(jnp.float32), chosen.astype(jnp.float32), precision=highest)

    near_field = lax.map(near_row, jnp.arange(strike_count, dtype=jnp.int32))

    moments = jnp.einsum("abkt,abte->abke", source_basis.astype(jnp.float32), slip_rate.astype(jnp.float32), precision=highest)
    carried = jnp.einsum("abkq,abqe->abke", leaf_up, moments, precision=highest)
    carried = carried.reshape(N_ROW, ALONG, N_COL, DIP, rank_width, member_count)
    node_moments = jnp.sum(carried, axis=(1, 3))
    for tree_level in range(CLEV):
        left_half = node_moments[:, 0::2]
        right_half = node_moments[:, 1::2]
        node_moments = jnp.einsum("rkq,rjqe->rjke", strip_up[:, tree_level, 0], left_half, precision=highest) + jnp.einsum("rkq,rjqe->rjke", strip_up[:, tree_level, 1], right_half, precision=highest)
    top_moments = node_moments[:, 0]

    strip_coeff = jnp.einsum("rakq,raqe->rke", coupling, top_moments[strip_lists], precision=highest)

    node_coeff = strip_coeff[:, None]
    for tree_level in reversed(range(CLEV)):
        first_child = jnp.einsum("rkq,rjqe->rjke", strip_down[:, tree_level, 0], node_coeff, precision=highest)
        second_child = jnp.einsum("rkq,rjqe->rjke", strip_down[:, tree_level, 1], node_coeff, precision=highest)
        node_coeff = jnp.stack([first_child, second_child], axis=2).reshape(N_ROW, -1, rank_width, member_count)
    spread = jnp.broadcast_to(node_coeff[:, None, :, None], (N_ROW, ALONG, N_COL, DIP, rank_width, member_count))
    spread = spread.reshape(strike_count, dip_count, rank_width, member_count)
    leaf_coeff = jnp.einsum("abkq,abqe->abke", leaf_down, spread, precision=highest).astype(jnp.bfloat16)
    far_field = jnp.einsum("abkt,abke->abte", target_basis.astype(jnp.float32), leaf_coeff.astype(jnp.float32), precision=highest)
    return (near_field + far_field).astype(jnp.bfloat16)
```

```python
import jax
import jax.numpy as jnp
from jax import lax
from jax.experimental import pallas as pl
from jax.experimental.pallas import tpu as pltpu
from jax.sharding import PartitionSpec as P

F32 = jnp.float32
BF16 = jnp.bfloat16
QUARTERS = 4


def halves(value):
    high = value.astype(BF16)
    return high, (value - high.astype(F32)).astype(BF16)


def dot(left, right):
    return jnp.dot(left, right, preferred_element_type=F32)


def dot_split(left, right):
    rows = left.shape[0]
    left_high, left_low = halves(left)
    right_high, right_low = halves(right)
    both = dot(jnp.concatenate([left_high, left_low], axis=0), right_high)
    return both[:rows] + both[rows:] + dot(left_high, right_low)


def chain_of(ref, col, levels):
    return [ref[level, (col >> level) & 1] for level in range(levels)]


def pack(tile, odd):
    half = tile.shape[0] // 2
    lane = lax.broadcasted_iota(jnp.int32, (half, tile.shape[1]), 1)
    left = lane < tile.shape[1] // 2
    upper, lower = tile[:half], tile[half:]
    shift = tile.shape[1] // 2
    if odd:
        return jnp.where(left, pltpu.roll(upper, shift, 1), lower)
    return jnp.where(left, upper, pltpu.roll(lower, shift, 1))


def fetch(refs, buffers, sems):
    copies = [
        pltpu.make_async_copy(ref, buffer, sems.at[at])
        for at, (ref, buffer) in enumerate(zip(refs, buffers, strict=True))
    ]
    for copy in copies:
        copy.start()
    return copies


def up_kernel(
    strip_up_ref, leaf_up_ref, basis_ref, slip_ref, out_ref, strip_up, leaf_up, basis, slip, sems
):
    leaves = slip_ref.shape[0]
    copies = fetch(
        (strip_up_ref, leaf_up_ref, basis_ref, slip_ref), (strip_up, leaf_up, basis, slip), sems
    )
    copies[0].wait()
    s0, s1, s2, s3 = chain_of(strip_up, lax.axis_index("col"), 4)
    chain = dot_split(dot_split(s3, s2), dot_split(s1, s0))
    copies[1].wait()
    ups = jnp.concatenate([leaf_up[leaf] for leaf in range(leaves)], axis=1)
    copies[2].wait()
    copies[3].wait()
    moments = jnp.concatenate([dot(basis[leaf], slip[leaf]) for leaf in range(leaves)], axis=0)
    node = dot_split(chain, dot_split(ups, moments))
    for quarter in range(QUARTERS):
        half = quarter // 2
        packed = pack(node[:, 128 * half : 128 * (half + 1)], quarter % 2).astype(BF16)
        for copy in range(out_ref.shape[0] // QUARTERS):
            out_ref[copy * QUARTERS + quarter] = packed


def sum_kernel(in_ref, before_ref, after_ref, out_ref):
    del before_ref, after_ref
    total = jnp.sum(in_ref[...].astype(F32), axis=0).astype(BF16)
    for copy in range(out_ref.shape[0]):
        out_ref[copy] = total


def weights_kernel(lists_ref, coupling_ref, after_ref, out_ref, coupling, wide, sems):
    del after_ref
    (copy,) = fetch((coupling_ref,), (coupling,), sems)
    strips, rank = coupling.shape[0], coupling.shape[1]
    half = rank // 2
    columns = out_ref.shape[1]
    row = lax.broadcasted_iota(jnp.int32, (half, columns), 0)
    column = lax.broadcasted_iota(jnp.int32, (half, columns), 1)
    chosen = [
        jnp.where(column == row + lists_ref[strip] * half, 1.0, 0.0).astype(BF16) for strip in range(strips)
    ]
    copy.wait()
    for strip in range(strips):
        at = slice(strip * half, (strip + 1) * half)
        wide[0:rank, at] = coupling[strip, :, 0:half]
        wide[rank : 2 * rank, at] = coupling[strip, :, half:rank]
    high, low = halves(wide[...])
    both = dot(jnp.concatenate([high, low], axis=0), jnp.concatenate(chosen, axis=0))
    out_ref[...] = both.astype(BF16)


def far_kernel(strip_down_ref, leaf_down_ref, target_ref, after_ref, out_ref, strip_down, leaf_down, target, sems):
    del after_ref
    for copy in fetch((strip_down_ref, leaf_down_ref, target_ref), (strip_down, leaf_down, target), sems):
        copy.wait()
    s0, s1, s2, s3 = chain_of(strip_down, lax.axis_index("col"), 4)
    chain = dot_split(dot_split(s0, s1), dot_split(s2, s3))
    leaves, rank, size = target.shape
    for leaf in range(leaves):
        down_high, down_low = halves(dot_split(leaf_down[leaf], chain))
        turned = target[leaf].astype(F32).T.astype(BF16)
        high, low = halves(dot(turned, down_high) + dot(turned, down_low))
        out_ref[leaf * size : (leaf + 1) * size, 0:rank] = high
        out_ref[leaf * size : (leaf + 1) * size, rank : 2 * rank] = low


def hold_kernel(blocks_ref, after_ref, out_ref, sems):
    del after_ref
    for copy in fetch((blocks_ref,), (out_ref,), sems):
        copy.wait()


def couple_kernel(tops_ref, weights_ref, out_ref):
    rank = weights_ref.shape[0] // 4
    half = rank // 2
    tops = tops_ref[...].reshape(tops_ref.shape[0] * tops_ref.shape[1], tops_ref.shape[2])
    product = dot(weights_ref[...], tops)
    product = product[: 2 * rank] + product[2 * rank :]
    upper, lower = product[:rank], product[rank:]
    lanes = product.shape[1]
    left = lax.broadcasted_iota(jnp.int32, (half, lanes), 1) < lanes // 2
    packed = jnp.where(
        left,
        upper[:half] + pltpu.roll(lower[:half], lanes // 2, 1),
        pltpu.roll(upper[half:], lanes // 2, 1) + lower[half:],
    ).astype(BF16)
    for copy in range(out_ref.shape[0]):
        out_ref[copy] = packed


def rim_kernel(slip_ref, before_ref, after_ref, after_sum_ref, left_ref, right_ref):
    del after_sum_ref
    along, dip = slip_ref.shape[0], slip_ref.shape[1]
    for ref, col in ((left_ref, 0), (right_ref, dip - 1)):
        ref[0] = before_ref[col]
        ref[along + 1] = after_ref[col]
        for row in range(along):
            ref[row + 1] = slip_ref[row, col]


def near_kernel(lists_ref, slip_ref, before_ref, after_ref, left_ref, right_ref, blocks_ref, out_ref, padded):
    along, dip, near = blocks_ref.shape[0], blocks_ref.shape[1], blocks_ref.shape[2]
    width = dip + 2
    for row in range(along + 2):
        padded[row * width] = left_ref[row]
        padded[row * width + width - 1] = right_ref[row]
    for col in range(dip):
        padded[1 + col] = before_ref[col]
        padded[(along + 1) * width + 1 + col] = after_ref[col]
        for row in range(along):
            padded[(row + 1) * width + 1 + col] = slip_ref[row, col]
    for row in range(along):
        for col in range(dip):
            leaf = row * dip + col
            sources = []
            for at in range(near):
                place = lists_ref[leaf * near + at]
                sources.append(padded[(row + place // 3) * width + col + place % 3])
            out_ref[leaf] = dot(
                jnp.concatenate([blocks_ref[row, col, at] for at in range(near)], axis=1),
                jnp.concatenate(sources, axis=0),
            )


def final_kernel(near_ref, far_ref, coeff_ref, out_ref, held, sems):
    leaves, size = held.shape[0], held.shape[1]
    rows, lanes = coeff_ref.shape[1], coeff_ref.shape[2]
    left = lax.broadcasted_iota(jnp.int32, (rows, lanes), 1) < lanes // 2
    tiles = []
    for half in range(2):
        one = coeff_ref[2 * half].astype(F32)
        two = coeff_ref[2 * half + 1].astype(F32)
        upper = jnp.where(left, one, pltpu.roll(two, lanes // 2, 1))
        lower = jnp.where(left, pltpu.roll(one, lanes // 2, 1), two)
        tiles.append(jnp.concatenate([upper, lower], axis=0).astype(BF16))
    coeff = jnp.concatenate(tiles, axis=1)
    coeff = jnp.concatenate([coeff, coeff], axis=0)
    copies = []
    for leaf in range(leaves):
        far = dot(far_ref[leaf * size : (leaf + 1) * size], coeff)
        held[leaf] = (near_ref[leaf] + far).astype(BF16)
        copy = pltpu.make_async_copy(held.at[leaf], out_ref.at[leaf], sems.at[leaf])
        copy.start()
        copies.append(copy)
    for copy in copies:
        copy.wait()


def call(kernel, outs, places, *args, to="v", scratch=(), name=None, flops=0, size=0):
    args = [pltpu.with_memory_space_constraint(a, pltpu.HBM) if p == "h" else a for p, a in zip(places, args, strict=True)]
    spaces = {"s": pltpu.SMEM, "v": pltpu.VMEM, "a": pl.ANY, "h": pltpu.HBM}
    return pl.pallas_call(
        kernel,
        out_shape=outs,
        in_specs=[pl.BlockSpec(memory_space=spaces[p]) for p in places],
        out_specs=jax.tree.map(lambda _: pl.BlockSpec(memory_space=spaces[to]), outs),
        scratch_shapes=scratch,
        compiler_params=pltpu.CompilerParams(vmem_limit_bytes=12 * 1024 * 1024),
        cost_estimate=pl.CostEstimate(flops=flops, bytes_accessed=size, transcendentals=0),
        name=name,
    )(*args)


def body(
    slip_rate,
    near_lists,
    near_blocks,
    source_basis,
    target_basis,
    leaf_up,
    leaf_down,
    strip_up,
    strip_down,
    strip_lists,
    coupling,
):
    along, dip, size, members = slip_rate.shape
    rank = source_basis.shape[2]
    leaves = along * dip
    n_row, n_col = lax.axis_size("row"), lax.axis_size("col")
    sds = jax.ShapeDtypeStruct
    slips = slip_rate.reshape(leaves, size, members)
    piece = (rank // 2, 128)

    dma = pltpu.SemaphoreType.DMA
    mega = 1024 * 1024
    basis = source_basis.reshape(leaves, rank, size)
    target = target_basis.reshape(leaves, rank, size)
    ups = leaf_up.reshape(leaves, rank, rank)
    downs = leaf_down.reshape(leaves, rank, rank)
    couplings = coupling[0]
    strips = couplings.shape[0]

    def room(value):
        return pltpu.VMEM(value.shape, value.dtype)

    parts = call(
        up_kernel,
        sds((n_col, *piece), BF16),
        "hhhh",
        strip_up[0],
        ups,
        basis,
        slips,
        scratch=[room(strip_up[0]), room(ups), room(basis), room(slips), dma((4,))],
        name="up",
        flops=100_000_000,
        size=2 * mega,
    )
    weights = call(
        weights_kernel,
        sds((4 * rank, n_row * rank // 2), BF16),
        "sha",
        strip_lists[0],
        couplings,
        parts,
        scratch=[room(couplings), pltpu.VMEM((2 * rank, strips * rank // 2), F32), dma((1,))],
        name="weights",
        flops=100_000_000,
        size=mega,
    )
    far = call(
        far_kernel,
        sds((leaves * size, 2 * rank), BF16),
        "hhha",
        strip_down[0],
        downs,
        target,
        parts,
        scratch=[room(strip_down[0]), room(downs), room(target), dma((3,))],
        name="far",
        flops=100_000_000,
        size=mega,
    )
    blocks = call(
        hold_kernel,
        sds(near_blocks.shape, BF16),
        "ha",
        near_blocks,
        parts,
        scratch=[dma((1,))],
        name="hold",
        flops=1_000_000,
        size=2 * mega,
    )
    held, _ = lax.optimization_barrier((slip_rate, weights))
    up_row = [(i, i + 1) for i in range(n_row - 1)]
    down_row = [(j, i) for i, j in up_row]
    up_col = [(i, i + 1) for i in range(n_col - 1)]
    down_col = [(j, i) for i, j in up_col]

    parts = lax.all_to_all(parts, "col", 0, 0, tiled=True)
    before = lax.ppermute(held[along - 1], "row", up_row)
    after = lax.ppermute(held[0], "row", down_row)
    tops = call(sum_kernel, sds((n_row, *piece), BF16), "vaa", parts, before, after, name="sum", flops=10_000_000, size=mega // 2)
    rim_left, rim_right = call(
        rim_kernel,
        (sds((along + 2, size, members), BF16), sds((along + 2, size, members), BF16)),
        "vvva",
        held,
        before,
        after,
        tops,
        name="rim",
        flops=1_000_000,
        size=mega,
    )
    tops = lax.all_to_all(tops, "row", 0, 0, tiled=True)
    from_left = lax.ppermute(rim_right, "col", up_col)
    from_right = lax.ppermute(rim_left, "col", down_col)
    coeff = call(
        couple_kernel,
        sds((QUARTERS, *piece), BF16),
        "vv",
        tops,
        weights,
        name="couple",
        flops=30_000_000_000,
        size=mega // 2,
    )
    groups = [list(range(i, i + QUARTERS)) for i in range(0, n_col, QUARTERS)]
    coeff = lax.all_to_all(coeff, "col", 0, 0, tiled=True, axis_index_groups=groups)
    near = call(
        near_kernel,
        sds((leaves, size, members), F32),
        "svvvvvv",
        near_lists.reshape(-1),
        held,
        before,
        after,
        from_left,
        from_right,
        blocks,
        scratch=[pltpu.VMEM(((along + 2) * (dip + 2), size, members), BF16)],
        name="near",
        flops=2 * leaves * 6 * size * size * members,
        size=4 * mega,
    )
    stress = call(
        final_kernel,
        sds((leaves, size, members), BF16),
        "vvv",
        near,
        far,
        coeff,
        to="a",
        scratch=[pltpu.VMEM((leaves, size, members), BF16), dma((leaves,))],
        name="final",
        flops=2 * leaves * size * members * rank * 2,
        size=2 * mega,
    )
    return stress.reshape(along, dip, size, members)


def solution(mesh):
    in_specs = (
        P("row", "col", None, None),
        P("row", "col", None),
        P("row", "col", None, None, None),
        P("row", "col", None, None),
        P("row", "col", None, None),
        P("row", "col", None, None),
        P("row", "col", None, None),
        P("row", None, None, None, None),
        P("row", None, None, None, None),
        P("row", None),
        P("row", None, None, None),
    )
    out_specs = P("row", "col", None, None)
    return jax.shard_map(body, mesh=mesh, in_specs=in_specs, out_specs=out_specs, check_vma=False)
```

```python
import jax
import jax.numpy as jnp
from jax import lax
from jax.experimental import pallas as pl
from jax.experimental.pallas import tpu as pltpu
from jax.sharding import PartitionSpec as P

F32 = jnp.float32
BF16 = jnp.bfloat16
QUARTERS = 4
COL_FIRST = 11
ROW_FIRST = 31


def halves(value):
    high = value.astype(BF16)
    return high, (value - high.astype(F32)).astype(BF16)


def dot(left, right):
    return jnp.dot(left, right, preferred_element_type=F32)


def dot_split(left, right):
    rows = left.shape[0]
    left_high, left_low = halves(left)
    right_high, right_low = halves(right)
    both = dot(jnp.concatenate([left_high, left_low], axis=0), right_high)
    return both[:rows] + both[rows:] + dot(left_high, right_low)


def chain_of(ref, col, levels):
    return [ref[level, (col >> level) & 1] for level in range(levels)]


def pack(tile, odd):
    half = tile.shape[0] // 2
    lane = lax.broadcasted_iota(jnp.int32, (half, tile.shape[1]), 1)
    left = lane < tile.shape[1] // 2
    upper, lower = tile[:half], tile[half:]
    shift = tile.shape[1] // 2
    if odd:
        return jnp.where(left, pltpu.roll(upper, shift, 1), lower)
    return jnp.where(left, upper, pltpu.roll(lower, shift, 1))


def fetch(refs, buffers, sems):
    copies = [
        pltpu.make_async_copy(ref, buffer, sems.at[at])
        for at, (ref, buffer) in enumerate(zip(refs, buffers, strict=True))
    ]
    for copy in copies:
        copy.start()
    return copies


def up_kernel(
    strip_up_ref, leaf_up_ref, basis_ref, slip_ref, out_ref, strip_up, leaf_up, basis, slip, sems
):
    leaves = slip_ref.shape[0]
    copies = fetch(
        (strip_up_ref, leaf_up_ref, basis_ref, slip_ref), (strip_up, leaf_up, basis, slip), sems
    )
    copies[0].wait()
    s0, s1, s2, s3 = chain_of(strip_up, lax.axis_index("col"), 4)
    chain = dot_split(dot_split(s3, s2), dot_split(s1, s0))
    copies[1].wait()
    ups = dot_split(chain, jnp.concatenate([leaf_up[leaf] for leaf in range(leaves)], axis=1))
    copies[2].wait()
    copies[3].wait()
    moments = jnp.concatenate([dot(basis[leaf], slip[leaf]) for leaf in range(leaves)], axis=0)
    node = dot_split(ups, moments)
    for quarter in range(QUARTERS):
        half = quarter // 2
        packed = pack(node[:, 128 * half : 128 * (half + 1)], quarter % 2).astype(BF16)
        for copy in range(out_ref.shape[0] // QUARTERS):
            out_ref[copy * QUARTERS + (quarter - COL_FIRST) % QUARTERS] = packed


def sum_kernel(in_ref, after_ref, out_ref):
    del after_ref
    total = jnp.sum(in_ref[...].astype(F32), axis=0).astype(BF16)
    for copy in range(out_ref.shape[0]):
        out_ref[copy] = total


def weights_kernel(lists_ref, coupling_ref, after_ref, out_ref, wide):
    del after_ref
    strips, rank = coupling_ref.shape[0], coupling_ref.shape[1]
    half = rank // 2
    columns = out_ref.shape[1]
    row = lax.broadcasted_iota(jnp.int32, (half, columns), 0)
    column = lax.broadcasted_iota(jnp.int32, (half, columns), 1)
    chosen = []
    for strip in range(strips):
        place = (ROW_FIRST - lists_ref[strip]) & (columns // half - 1)
        chosen.append(jnp.where(column == row + place * half, 1.0, 0.0).astype(BF16))
    for strip in range(strips):
        at = slice(strip * half, (strip + 1) * half)
        wide[0:rank, at] = coupling_ref[strip, :, 0:half]
        wide[rank : 2 * rank, at] = coupling_ref[strip, :, half:rank]
    high, low = halves(wide[...])
    both = dot(jnp.concatenate([high, low], axis=0), jnp.concatenate(chosen, axis=0))
    out_ref[...] = both.astype(BF16)


def far_kernel(strip_down, leaf_down, target, after_ref, out_ref):
    del after_ref
    s0, s1, s2, s3 = chain_of(strip_down, lax.axis_index("col"), 4)
    chain = dot_split(dot_split(s0, s1), dot_split(s2, s3))
    leaves, rank, size = target.shape
    for leaf in range(leaves):
        down_high, down_low = halves(dot_split(leaf_down[leaf], chain))
        turned = target[leaf].astype(F32).T.astype(BF16)
        high, low = halves(dot(turned, down_high) + dot(turned, down_low))
        out_ref[leaf * size : (leaf + 1) * size, 0:rank] = high
        out_ref[leaf * size : (leaf + 1) * size, rank : 2 * rank] = low


def hold_kernel(blocks_ref, after_ref, out_ref, sems):
    del after_ref
    for copy in fetch((blocks_ref,), (out_ref,), sems):
        copy.wait()


def couple_kernel(tops_ref, weights_ref, out_ref):
    rank = weights_ref.shape[0] // 4
    half = rank // 2
    tops = tops_ref[...].reshape(tops_ref.shape[0] * tops_ref.shape[1], tops_ref.shape[2])
    product = dot(weights_ref[...], tops)
    product = product[: 2 * rank] + product[2 * rank :]
    upper, lower = product[:rank], product[rank:]
    lanes = product.shape[1]
    left = lax.broadcasted_iota(jnp.int32, (half, lanes), 1) < lanes // 2
    packed = jnp.where(
        left,
        upper[:half] + pltpu.roll(lower[:half], lanes // 2, 1),
        pltpu.roll(upper[half:], lanes // 2, 1) + lower[half:],
    ).astype(BF16)
    for copy in range(out_ref.shape[0]):
        out_ref[copy] = packed


def edges_kernel(slip_ref, after_ref, first_ref, last_ref):
    del after_ref
    first_ref[...] = slip_ref[0]
    last_ref[...] = slip_ref[slip_ref.shape[0] - 1]


def rim_kernel(slip_ref, before_ref, after_ref, after_sum_ref, left_ref, right_ref):
    del after_sum_ref
    along, dip = slip_ref.shape[0], slip_ref.shape[1]
    for ref, col in ((left_ref, 0), (right_ref, dip - 1)):
        ref[0] = before_ref[col]
        ref[along + 1] = after_ref[col]
        for row in range(along):
            ref[row + 1] = slip_ref[row, col]


def near_kernel(lists_ref, slip_ref, before_ref, after_ref, left_ref, right_ref, blocks_ref, out_ref, padded):
    along, dip, near = blocks_ref.shape[0], blocks_ref.shape[1], blocks_ref.shape[2]
    width = dip + 2
    for row in range(along + 2):
        padded[row * width] = left_ref[row]
        padded[row * width + width - 1] = right_ref[row]
    for col in range(dip):
        padded[1 + col] = before_ref[col]
        padded[(along + 1) * width + 1 + col] = after_ref[col]
        for row in range(along):
            padded[(row + 1) * width + 1 + col] = slip_ref[row, col]
    for row in range(along):
        for col in range(dip):
            leaf = row * dip + col
            sources = []
            for at in range(near):
                place = lists_ref[leaf * near + at]
                sources.append(padded[(row + place // 3) * width + col + place % 3])
            out_ref[leaf] = dot(
                jnp.concatenate([blocks_ref[row, col, at] for at in range(near)], axis=1),
                jnp.concatenate(sources, axis=0),
            )


def final_kernel(near_ref, far_ref, coeff_ref, out_ref, held, sems):
    leaves, size = held.shape[0], held.shape[1]
    rows, lanes = coeff_ref.shape[1], coeff_ref.shape[2]
    left = lax.broadcasted_iota(jnp.int32, (rows, lanes), 1) < lanes // 2
    tiles = []
    for half in range(2):
        one = coeff_ref[QUARTERS - 1 - 2 * half].astype(F32)
        two = coeff_ref[QUARTERS - 2 - 2 * half].astype(F32)
        upper = jnp.where(left, one, pltpu.roll(two, lanes // 2, 1))
        lower = jnp.where(left, pltpu.roll(one, lanes // 2, 1), two)
        tiles.append(jnp.concatenate([upper, lower], axis=0).astype(BF16))
    coeff = jnp.concatenate(tiles, axis=1)
    coeff = jnp.concatenate([coeff, coeff], axis=0)
    copies = []
    for leaf in range(leaves):
        far = dot(far_ref[leaf * size : (leaf + 1) * size], coeff)
        held[leaf] = (near_ref[leaf] + far).astype(BF16)
        copy = pltpu.make_async_copy(held.at[leaf], out_ref.at[leaf], sems.at[leaf])
        copy.start()
        copies.append(copy)
    for copy in copies:
        copy.wait()


def call(kernel, outs, places, *args, to="v", scratch=(), name=None, flops=0, size=0):
    args = [pltpu.with_memory_space_constraint(a, pltpu.HBM) if p == "h" else a for p, a in zip(places, args, strict=True)]
    spaces = {"s": pltpu.SMEM, "v": pltpu.VMEM, "a": pl.ANY, "h": pltpu.HBM}
    return pl.pallas_call(
        kernel,
        out_shape=outs,
        in_specs=[pl.BlockSpec(memory_space=spaces[p]) for p in places],
        out_specs=jax.tree.map(lambda _: pl.BlockSpec(memory_space=spaces[to]), outs),
        scratch_shapes=scratch,
        compiler_params=pltpu.CompilerParams(vmem_limit_bytes=12 * 1024 * 1024),
        cost_estimate=pl.CostEstimate(flops=flops, bytes_accessed=size, transcendentals=0),
        name=name,
    )(*args)


def body(
    slip_rate,
    near_lists,
    near_blocks,
    source_basis,
    target_basis,
    leaf_up,
    leaf_down,
    strip_up,
    strip_down,
    strip_lists,
    coupling,
):
    along, dip, size, members = slip_rate.shape
    rank = source_basis.shape[2]
    leaves = along * dip
    n_row, n_col = lax.axis_size("row"), lax.axis_size("col")
    sds = jax.ShapeDtypeStruct
    slips = slip_rate.reshape(leaves, size, members)
    piece = (rank // 2, 128)

    dma = pltpu.SemaphoreType.DMA
    mega = 1024 * 1024
    basis = source_basis.reshape(leaves, rank, size)
    target = target_basis.reshape(leaves, rank, size)
    ups = leaf_up.reshape(leaves, rank, rank)
    downs = leaf_down.reshape(leaves, rank, rank)
    couplings = coupling[0]
    strips = couplings.shape[0]

    def room(value):
        return pltpu.VMEM(value.shape, value.dtype)

    parts = call(
        up_kernel,
        sds((n_col, *piece), BF16),
        "hhhh",
        strip_up[0],
        ups,
        basis,
        slips,
        scratch=[room(strip_up[0]), room(ups), room(basis), room(slips), dma((4,))],
        name="up",
        flops=100_000_000,
        size=2 * mega,
    )
    up_row = [(i, i + 1) for i in range(n_row - 1)]
    down_row = [(j, i) for i, j in up_row]
    up_col = [(i, i + 1) for i in range(n_col - 1)]
    down_col = [(j, i) for i, j in up_col]

    edge = sds((dip, size, members), BF16)
    first, last = call(
        edges_kernel,
        (edge, edge),
        "va",
        slip_rate,
        parts,
        name="edges",
        flops=10_000_000_000,
        size=mega,
    )
    before = lax.ppermute(last, "row", up_row)
    after = lax.ppermute(first, "row", down_row)
    turned = [(i + COL_FIRST) % n_col for i in range(n_col)]
    parts = lax.all_to_all(parts, "col", 0, 0, tiled=True, axis_index_groups=[turned])
    tops = call(sum_kernel, sds((n_row, *piece), BF16), "va", parts, first, name="sum", flops=30_000_000_000, size=mega // 2)
    rim_left, rim_right = call(
        rim_kernel,
        (sds((along + 2, size, members), BF16), sds((along + 2, size, members), BF16)),
        "vvva",
        slip_rate,
        before,
        after,
        tops,
        name="rim",
        flops=1_000_000,
        size=mega,
    )
    weights = call(
        weights_kernel,
        sds((4 * rank, n_row * rank // 2), BF16),
        "sva",
        strip_lists[0],
        couplings,
        rim_left,
        scratch=[pltpu.VMEM((2 * rank, strips * rank // 2), F32)],
        name="weights",
        flops=30_000_000_000,
        size=mega,
    )
    order = [(ROW_FIRST - i) % n_row for i in range(n_row)]
    tops = lax.all_to_all(tops, "row", 0, 0, tiled=True, axis_index_groups=[order])
    from_left = lax.ppermute(rim_right, "col", up_col)
    from_right = lax.ppermute(rim_left, "col", down_col)
    coeff = call(
        couple_kernel,
        sds((QUARTERS, *piece), BF16),
        "vv",
        tops,
        weights,
        name="couple",
        flops=30_000_000_000,
        size=mega // 2,
    )
    far = call(
        far_kernel,
        sds((leaves * size, 2 * rank), BF16),
        "vvva",
        strip_down[0],
        downs,
        target,
        coeff,
        name="far",
        flops=100_000_000,
        size=mega,
    )
    blocks = call(
        hold_kernel,
        sds(near_blocks.shape, BF16),
        "ha",
        near_blocks,
        coeff,
        scratch=[dma((1,))],
        name="hold",
        flops=1_000_000,
        size=2 * mega,
    )
    groups = [list(range(i, i + QUARTERS))[::-1] for i in range(0, n_col, QUARTERS)]
    coeff = lax.all_to_all(coeff, "col", 0, 0, tiled=True, axis_index_groups=groups)
    near = call(
        near_kernel,
        sds((leaves, size, members), F32),
        "svvvvvv",
        near_lists.reshape(-1),
        slip_rate,
        before,
        after,
        from_left,
        from_right,
        blocks,
        scratch=[pltpu.VMEM(((along + 2) * (dip + 2), size, members), BF16)],
        name="near",
        flops=2 * leaves * 6 * size * size * members,
        size=4 * mega,
    )
    stress = call(
        final_kernel,
        sds((leaves, size, members), BF16),
        "vvv",
        near,
        far,
        coeff,
        to="a",
        scratch=[pltpu.VMEM((leaves, size, members), BF16), dma((leaves,))],
        name="final",
        flops=2 * leaves * size * members * rank * 2,
        size=2 * mega,
    )
    return stress.reshape(along, dip, size, members)


def solution(mesh):
    in_specs = (
        P("row", "col", None, None),
        P("row", "col", None),
        P("row", "col", None, None, None),
        P("row", "col", None, None),
        P("row", "col", None, None),
        P("row", "col", None, None),
        P("row", "col", None, None),
        P("row", None, None, None, None),
        P("row", None, None, None, None),
        P("row", None),
        P("row", None, None, None),
    )
    out_specs = P("row", "col", None, None)
    return jax.shard_map(body, mesh=mesh, in_specs=in_specs, out_specs=out_specs, check_vma=False)
```

```python
import jax
import jax.numpy as jnp
from jax import lax
from jax.experimental import pallas as pl
from jax.experimental.pallas import tpu as pltpu
from jax.sharding import PartitionSpec as P

F32 = jnp.float32
BF16 = jnp.bfloat16
QUARTERS = 4
COL_ORDER = (11, 0, 1, 2, 3, 4, 5, 6, 7, 15, 14, 13, 12, 10, 9, 8)
ROW_FIRST = 31


def halves(value):
    high = value.astype(BF16)
    return high, (value - high.astype(F32)).astype(BF16)


def dot(left, right):
    return jnp.dot(left, right, preferred_element_type=F32)


def dot_split(left, right):
    rows = left.shape[0]
    left_high, left_low = halves(left)
    right_high, right_low = halves(right)
    both = dot(jnp.concatenate([left_high, left_low], axis=0), right_high)
    return both[:rows] + both[rows:] + dot(left_high, right_low)


def chain_of(ref, col, levels):
    return [ref[level, (col >> level) & 1] for level in range(levels)]


def pack(tile, odd):
    half = tile.shape[0] // 2
    lane = lax.broadcasted_iota(jnp.int32, (half, tile.shape[1]), 1)
    left = lane < tile.shape[1] // 2
    upper, lower = tile[:half], tile[half:]
    shift = tile.shape[1] // 2
    if odd:
        return jnp.where(left, pltpu.roll(upper, shift, 1), lower)
    return jnp.where(left, upper, pltpu.roll(lower, shift, 1))


def fetch(refs, buffers, sems):
    copies = [
        pltpu.make_async_copy(ref, buffer, sems.at[at])
        for at, (ref, buffer) in enumerate(zip(refs, buffers, strict=True))
    ]
    for copy in copies:
        copy.start()
    return copies


def up_kernel(
    strip_up_ref, leaf_up_ref, basis_ref, slip_ref, out_ref, strip_up, leaf_up, basis, slip, sems
):
    leaves, levels = slip_ref.shape[0], strip_up.shape[0]
    col = lax.axis_index("col")
    copies = fetch(
        [strip_up_ref.at[level, (col >> level) & 1] for level in range(levels)]
        + [leaf_up_ref, basis_ref, slip_ref],
        [strip_up.at[level] for level in range(levels)] + [leaf_up, basis, slip],
        sems,
    )
    for copy in copies[:levels]:
        copy.wait()
    chain = dot_split(dot_split(strip_up[3], strip_up[2]), dot_split(strip_up[1], strip_up[0]))
    copies[levels].wait()
    ups = dot_split(chain, jnp.concatenate([leaf_up[leaf] for leaf in range(leaves)], axis=1))
    copies[levels + 1].wait()
    copies[levels + 2].wait()
    moments = jnp.concatenate([dot(basis[leaf], slip[leaf]) for leaf in range(leaves)], axis=0)
    node = dot_split(ups, moments)
    for quarter in range(QUARTERS):
        half = quarter // 2
        packed = pack(node[:, 128 * half : 128 * (half + 1)], quarter % 2).astype(BF16)
        for at, place in enumerate(COL_ORDER):
            if place % QUARTERS == quarter:
                out_ref[at] = packed


def sum_kernel(in_ref, after_ref, out_ref):
    del after_ref
    total = jnp.sum(in_ref[...].astype(F32), axis=0).astype(BF16)
    for copy in range(out_ref.shape[0]):
        out_ref[copy] = total


def weights_kernel(lists_ref, coupling_ref, after_ref, out_ref, wide):
    del after_ref
    strips, rank = coupling_ref.shape[0], coupling_ref.shape[1]
    half = rank // 2
    columns = out_ref.shape[1]
    row = lax.broadcasted_iota(jnp.int32, (half, columns), 0)
    column = lax.broadcasted_iota(jnp.int32, (half, columns), 1)
    chosen = []
    for strip in range(strips):
        place = (ROW_FIRST - lists_ref[strip]) & (columns // half - 1)
        chosen.append(jnp.where(column == row + place * half, 1.0, 0.0).astype(BF16))
    for strip in range(strips):
        at = slice(strip * half, (strip + 1) * half)
        wide[0:rank, at] = coupling_ref[strip, :, 0:half]
        wide[rank : 2 * rank, at] = coupling_ref[strip, :, half:rank]
    high, low = halves(wide[...])
    both = dot(jnp.concatenate([high, low], axis=0), jnp.concatenate(chosen, axis=0))
    out_ref[...] = both.astype(BF16)


def far_kernel(strip_down, leaf_down, target, after_ref, out_ref):
    del after_ref
    s0, s1, s2, s3 = chain_of(strip_down, lax.axis_index("col"), 4)
    chain = dot_split(dot_split(s0, s1), dot_split(s2, s3))
    leaves, rank, size = target.shape
    for leaf in range(leaves):
        down_high, down_low = halves(dot_split(leaf_down[leaf], chain))
        turned = target[leaf].astype(F32).T.astype(BF16)
        high, low = halves(dot(turned, down_high) + dot(turned, down_low))
        out_ref[leaf * size : (leaf + 1) * size, 0:rank] = high
        out_ref[leaf * size : (leaf + 1) * size, rank : 2 * rank] = low


def hold_kernel(blocks_ref, after_ref, out_ref, sems):
    del after_ref
    for copy in fetch((blocks_ref,), (out_ref,), sems):
        copy.wait()


def couple_kernel(tops_ref, weights_ref, out_ref):
    rank = weights_ref.shape[0] // 4
    half = rank // 2
    tops = tops_ref[...].reshape(tops_ref.shape[0] * tops_ref.shape[1], tops_ref.shape[2])
    product = dot(weights_ref[...], tops)
    product = product[: 2 * rank] + product[2 * rank :]
    upper, lower = product[:rank], product[rank:]
    lanes = product.shape[1]
    left = lax.broadcasted_iota(jnp.int32, (half, lanes), 1) < lanes // 2
    packed = jnp.where(
        left,
        upper[:half] + pltpu.roll(lower[:half], lanes // 2, 1),
        pltpu.roll(upper[half:], lanes // 2, 1) + lower[half:],
    ).astype(BF16)
    for copy in range(out_ref.shape[0]):
        out_ref[copy] = packed


def edges_kernel(slip_ref, after_ref, first_ref, last_ref):
    del after_ref
    first_ref[...] = slip_ref[0]
    last_ref[...] = slip_ref[slip_ref.shape[0] - 1]


def rim_kernel(slip_ref, before_ref, after_ref, after_sum_ref, left_ref, right_ref):
    del after_sum_ref
    along, dip = slip_ref.shape[0], slip_ref.shape[1]
    for ref, col in ((left_ref, 0), (right_ref, dip - 1)):
        ref[0] = before_ref[col]
        ref[along + 1] = after_ref[col]
        for row in range(along):
            ref[row + 1] = slip_ref[row, col]


def near_kernel(lists_ref, slip_ref, before_ref, after_ref, left_ref, right_ref, blocks_ref, out_ref, padded):
    along, dip, near = blocks_ref.shape[0], blocks_ref.shape[1], blocks_ref.shape[2]
    width = dip + 2
    for row in range(along + 2):
        padded[row * width] = left_ref[row]
        padded[row * width + width - 1] = right_ref[row]
    for col in range(dip):
        padded[1 + col] = before_ref[col]
        padded[(along + 1) * width + 1 + col] = after_ref[col]
        for row in range(along):
            padded[(row + 1) * width + 1 + col] = slip_ref[row, col]
    for row in range(along):
        for col in range(dip):
            leaf = row * dip + col
            sources = []
            for at in range(near):
                place = lists_ref[leaf * near + at]
                sources.append(padded[(row + place // 3) * width + col + place % 3])
            out_ref[leaf] = dot(
                jnp.concatenate([blocks_ref[row, col, at] for at in range(near)], axis=1),
                jnp.concatenate(sources, axis=0),
            )


def final_kernel(near_ref, far_ref, coeff_ref, out_ref, held, sems):
    leaves, size = held.shape[0], held.shape[1]
    rows, lanes = coeff_ref.shape[1], coeff_ref.shape[2]
    left = lax.broadcasted_iota(jnp.int32, (rows, lanes), 1) < lanes // 2
    tiles = []
    for half in range(2):
        one = coeff_ref[QUARTERS - 1 - 2 * half].astype(F32)
        two = coeff_ref[QUARTERS - 2 - 2 * half].astype(F32)
        upper = jnp.where(left, one, pltpu.roll(two, lanes // 2, 1))
        lower = jnp.where(left, pltpu.roll(one, lanes // 2, 1), two)
        tiles.append(jnp.concatenate([upper, lower], axis=0).astype(BF16))
    coeff = jnp.concatenate(tiles, axis=1)
    coeff = jnp.concatenate([coeff, coeff], axis=0)
    copies = []
    for leaf in range(leaves):
        far = dot(far_ref[leaf * size : (leaf + 1) * size], coeff)
        held[leaf] = (near_ref[leaf] + far).astype(BF16)
        copy = pltpu.make_async_copy(held.at[leaf], out_ref.at[leaf], sems.at[leaf])
        copy.start()
        copies.append(copy)
    for copy in copies:
        copy.wait()


def call(kernel, outs, places, *args, to="v", scratch=(), name=None, flops=0, size=0):
    args = [pltpu.with_memory_space_constraint(a, pltpu.HBM) if p == "h" else a for p, a in zip(places, args, strict=True)]
    spaces = {"s": pltpu.SMEM, "v": pltpu.VMEM, "a": pl.ANY, "h": pltpu.HBM}
    return pl.pallas_call(
        kernel,
        out_shape=outs,
        in_specs=[pl.BlockSpec(memory_space=spaces[p]) for p in places],
        out_specs=jax.tree.map(lambda _: pl.BlockSpec(memory_space=spaces[to]), outs),
        scratch_shapes=scratch,
        compiler_params=pltpu.CompilerParams(vmem_limit_bytes=12 * 1024 * 1024),
        cost_estimate=pl.CostEstimate(flops=flops, bytes_accessed=size, transcendentals=0),
        name=name,
    )(*args)


def body(
    slip_rate,
    near_lists,
    near_blocks,
    source_basis,
    target_basis,
    leaf_up,
    leaf_down,
    strip_up,
    strip_down,
    strip_lists,
    coupling,
):
    along, dip, size, members = slip_rate.shape
    rank = source_basis.shape[2]
    leaves = along * dip
    n_row, n_col = lax.axis_size("row"), lax.axis_size("col")
    sds = jax.ShapeDtypeStruct
    slips = slip_rate.reshape(leaves, size, members)
    piece = (rank // 2, 128)

    dma = pltpu.SemaphoreType.DMA
    mega = 1024 * 1024
    basis = source_basis.reshape(leaves, rank, size)
    target = target_basis.reshape(leaves, rank, size)
    ups = leaf_up.reshape(leaves, rank, rank)
    downs = leaf_down.reshape(leaves, rank, rank)
    couplings = coupling[0]
    strips = couplings.shape[0]

    def room(value):
        return pltpu.VMEM(value.shape, value.dtype)

    parts = call(
        up_kernel,
        sds((n_col, *piece), BF16),
        "hhhh",
        strip_up[0],
        ups,
        basis,
        slips,
        scratch=[room(strip_up[0, :, 0]), room(ups), room(basis), room(slips), dma((strip_up.shape[1] + 3,))],
        name="up",
        flops=100_000_000,
        size=2 * mega,
    )
    up_row = [(i, i + 1) for i in range(n_row - 1)]
    down_row = [(j, i) for i, j in up_row]
    up_col = [(i, i + 1) for i in range(n_col - 1)]
    down_col = [(j, i) for i, j in up_col]

    edge = sds((dip, size, members), BF16)
    first, last = call(
        edges_kernel,
        (edge, edge),
        "va",
        slip_rate,
        parts,
        name="edges",
        flops=10_000_000_000,
        size=mega,
    )
    before = lax.ppermute(last, "row", up_row)
    after = lax.ppermute(first, "row", down_row)
    weights = call(
        weights_kernel,
        sds((4 * rank, n_row * rank // 2), BF16),
        "sva",
        strip_lists[0],
        couplings,
        first,
        scratch=[pltpu.VMEM((2 * rank, strips * rank // 2), F32)],
        name="weights",
        flops=100_000_000,
        size=mega,
    )
    parts = lax.all_to_all(parts, "col", 0, 0, tiled=True, axis_index_groups=[list(COL_ORDER)])
    tops = call(sum_kernel, sds((n_row, *piece), BF16), "va", parts, weights, name="sum", flops=30_000_000_000, size=mega // 2)
    rim_left, rim_right = call(
        rim_kernel,
        (sds((along + 2, size, members), BF16), sds((along + 2, size, members), BF16)),
        "vvva",
        slip_rate,
        before,
        after,
        tops,
        name="rim",
        flops=30_000_000_000,
        size=mega,
    )
    order = [(ROW_FIRST - i) % n_row for i in range(n_row)]
    tops = lax.all_to_all(tops, "row", 0, 0, tiled=True, axis_index_groups=[order])
    from_left = lax.ppermute(rim_right, "col", up_col)
    from_right = lax.ppermute(rim_left, "col", down_col)
    coeff = call(
        couple_kernel,
        sds((QUARTERS, *piece), BF16),
        "vv",
        tops,
        weights,
        name="couple",
        flops=30_000_000_000,
        size=mega // 2,
    )
    far = call(
        far_kernel,
        sds((leaves * size, 2 * rank), BF16),
        "vvva",
        strip_down[0],
        downs,
        target,
        coeff,
        name="far",
        flops=100_000_000,
        size=mega,
    )
    blocks = call(
        hold_kernel,
        sds(near_blocks.shape, BF16),
        "ha",
        near_blocks,
        coeff,
        scratch=[dma((1,))],
        name="hold",
        flops=1_000_000,
        size=2 * mega,
    )
    groups = [list(range(i, i + QUARTERS))[::-1] for i in range(0, n_col, QUARTERS)]
    coeff = lax.all_to_all(coeff, "col", 0, 0, tiled=True, axis_index_groups=groups)
    near = call(
        near_kernel,
        sds((leaves, size, members), F32),
        "svvvvvv",
        near_lists.reshape(-1),
        slip_rate,
        before,
        after,
        from_left,
        from_right,
        blocks,
        scratch=[pltpu.VMEM(((along + 2) * (dip + 2), size, members), BF16)],
        name="near",
        flops=2 * leaves * 6 * size * size * members,
        size=4 * mega,
    )
    stress = call(
        final_kernel,
        sds((leaves, size, members), BF16),
        "vvv",
        near,
        far,
        coeff,
        to="a",
        scratch=[pltpu.VMEM((leaves, size, members), BF16), dma((leaves,))],
        name="final",
        flops=2 * leaves * size * members * rank * 2,
        size=2 * mega,
    )
    return stress.reshape(along, dip, size, members)


def solution(mesh):
    in_specs = (
        P("row", "col", None, None),
        P("row", "col", None),
        P("row", "col", None, None, None),
        P("row", "col", None, None),
        P("row", "col", None, None),
        P("row", "col", None, None),
        P("row", "col", None, None),
        P("row", None, None, None, None),
        P("row", None, None, None, None),
        P("row", None),
        P("row", None, None, None),
    )
    out_specs = P("row", "col", None, None)
    return jax.shard_map(body, mesh=mesh, in_specs=in_specs, out_specs=out_specs, check_vma=False)
```

```python
import jax
import jax.numpy as jnp
from jax import lax
from jax.experimental import pallas as pl
from jax.experimental.pallas import tpu as pltpu
from jax.sharding import PartitionSpec as P

F32 = jnp.float32
BF16 = jnp.bfloat16
QUARTERS = 4
COL_ORDER = (11, 0, 1, 2, 3, 4, 5, 6, 7, 15, 14, 13, 12, 10, 9, 8)
ROW_FIRST = 21
GROUP_ORDER = (2, 3, 1, 0)


def halves(value):
    high = value.astype(BF16)
    return high, (value - high.astype(F32)).astype(BF16)


def dot(left, right):
    return jnp.dot(left, right, preferred_element_type=F32)


def dot_split(left, right):
    rows = left.shape[0]
    left_high, left_low = halves(left)
    right_high, right_low = halves(right)
    both = dot(jnp.concatenate([left_high, left_low], axis=0), right_high)
    return both[:rows] + both[rows:] + dot(left_high, right_low)


def chain_of(ref, col, levels):
    return [ref[level, (col >> level) & 1] for level in range(levels)]


def pack(tile, odd):
    half = tile.shape[0] // 2
    lane = lax.broadcasted_iota(jnp.int32, (half, tile.shape[1]), 1)
    left = lane < tile.shape[1] // 2
    upper, lower = tile[:half], tile[half:]
    shift = tile.shape[1] // 2
    if odd:
        return jnp.where(left, pltpu.roll(upper, shift, 1), lower)
    return jnp.where(left, upper, pltpu.roll(lower, shift, 1))


def fetch(refs, buffers, sems):
    copies = [
        pltpu.make_async_copy(ref, buffer, sems.at[at])
        for at, (ref, buffer) in enumerate(zip(refs, buffers, strict=True))
    ]
    for copy in copies:
        copy.start()
    return copies


def up_kernel(
    strip_up_ref, leaf_up_ref, basis_ref, slip_ref, out_ref, strip_up, leaf_up, basis, slip, sems
):
    leaves, levels = slip_ref.shape[0], strip_up.shape[0]
    col = lax.axis_index("col")
    copies = fetch(
        [strip_up_ref.at[level, (col >> level) & 1] for level in range(levels)]
        + [leaf_up_ref, basis_ref, slip_ref],
        [strip_up.at[level] for level in range(levels)] + [leaf_up, basis, slip],
        sems,
    )
    for copy in copies[:levels]:
        copy.wait()
    chain = dot_split(dot_split(strip_up[3], strip_up[2]), dot_split(strip_up[1], strip_up[0]))
    copies[levels].wait()
    ups = dot_split(chain, jnp.concatenate([leaf_up[leaf] for leaf in range(leaves)], axis=1))
    copies[levels + 1].wait()
    copies[levels + 2].wait()
    moments = jnp.concatenate([dot(basis[leaf], slip[leaf]) for leaf in range(leaves)], axis=0)
    node = dot_split(ups, moments)
    for quarter in range(QUARTERS):
        half = quarter // 2
        packed = pack(node[:, 128 * half : 128 * (half + 1)], quarter % 2).astype(BF16)
        for at, place in enumerate(COL_ORDER):
            if place % QUARTERS == quarter:
                out_ref[at] = packed


def sum_kernel(in_ref, after_ref, out_ref):
    del after_ref
    total = jnp.sum(in_ref[...].astype(F32), axis=0).astype(BF16)
    for copy in range(out_ref.shape[0]):
        out_ref[copy] = total


def weights_kernel(lists_ref, coupling_ref, after_ref, out_ref, wide):
    del after_ref
    strips, rank = coupling_ref.shape[0], coupling_ref.shape[1]
    half = rank // 2
    columns = out_ref.shape[1]
    row = lax.broadcasted_iota(jnp.int32, (half, columns), 0)
    column = lax.broadcasted_iota(jnp.int32, (half, columns), 1)
    chosen = []
    for strip in range(strips):
        place = (ROW_FIRST - lists_ref[strip]) & (columns // half - 1)
        chosen.append(jnp.where(column == row + place * half, 1.0, 0.0).astype(BF16))
    for strip in range(strips):
        at = slice(strip * half, (strip + 1) * half)
        wide[0:rank, at] = coupling_ref[strip, :, 0:half]
        wide[rank : 2 * rank, at] = coupling_ref[strip, :, half:rank]
    high, low = halves(wide[...])
    both = dot(jnp.concatenate([high, low], axis=0), jnp.concatenate(chosen, axis=0))
    out_ref[...] = both.astype(BF16)


def far_kernel(strip_down, leaf_down, target, after_ref, out_ref):
    del after_ref
    s0, s1, s2, s3 = chain_of(strip_down, lax.axis_index("col"), 4)
    chain = dot_split(dot_split(s0, s1), dot_split(s2, s3))
    leaves, rank, size = target.shape
    for leaf in range(leaves):
        down_high, down_low = halves(dot_split(leaf_down[leaf], chain))
        turned = target[leaf].astype(F32).T.astype(BF16)
        high, low = halves(dot(turned, down_high) + dot(turned, down_low))
        out_ref[leaf * size : (leaf + 1) * size, 0:rank] = high
        out_ref[leaf * size : (leaf + 1) * size, rank : 2 * rank] = low


def hold_kernel(blocks_ref, after_ref, out_ref, sems):
    del after_ref
    for copy in fetch((blocks_ref,), (out_ref,), sems):
        copy.wait()


def couple_kernel(tops_ref, weights_ref, out_ref):
    rank = weights_ref.shape[0] // 4
    half = rank // 2
    tops = tops_ref[...].reshape(tops_ref.shape[0] * tops_ref.shape[1], tops_ref.shape[2])
    product = dot(weights_ref[...], tops)
    product = product[: 2 * rank] + product[2 * rank :]
    upper, lower = product[:rank], product[rank:]
    lanes = product.shape[1]
    left = lax.broadcasted_iota(jnp.int32, (half, lanes), 1) < lanes // 2
    packed = jnp.where(
        left,
        upper[:half] + pltpu.roll(lower[:half], lanes // 2, 1),
        pltpu.roll(upper[half:], lanes // 2, 1) + lower[half:],
    ).astype(BF16)
    for copy in range(out_ref.shape[0]):
        out_ref[copy] = packed


def edges_kernel(slip_ref, after_ref, first_ref, last_ref):
    del after_ref
    first_ref[...] = slip_ref[0]
    last_ref[...] = slip_ref[slip_ref.shape[0] - 1]


def rim_kernel(slip_ref, before_ref, after_ref, after_sum_ref, left_ref, right_ref):
    del after_sum_ref
    along, dip = slip_ref.shape[0], slip_ref.shape[1]
    for ref, col in ((left_ref, 0), (right_ref, dip - 1)):
        ref[0] = before_ref[col]
        ref[along + 1] = after_ref[col]
        for row in range(along):
            ref[row + 1] = slip_ref[row, col]


def near_kernel(lists_ref, slip_ref, before_ref, after_ref, left_ref, right_ref, blocks_ref, out_ref, padded):
    along, dip, near = blocks_ref.shape[0], blocks_ref.shape[1], blocks_ref.shape[2]
    width = dip + 2
    for row in range(along + 2):
        padded[row * width] = left_ref[row]
        padded[row * width + width - 1] = right_ref[row]
    for col in range(dip):
        padded[1 + col] = before_ref[col]
        padded[(along + 1) * width + 1 + col] = after_ref[col]
        for row in range(along):
            padded[(row + 1) * width + 1 + col] = slip_ref[row, col]
    for row in range(along):
        for col in range(dip):
            leaf = row * dip + col
            sources = []
            for at in range(near):
                place = lists_ref[leaf * near + at]
                sources.append(padded[(row + place // 3) * width + col + place % 3])
            out_ref[leaf] = dot(
                jnp.concatenate([blocks_ref[row, col, at] for at in range(near)], axis=1),
                jnp.concatenate(sources, axis=0),
            )


def final_kernel(near_ref, far_ref, coeff_ref, out_ref, held, sems):
    leaves, size = held.shape[0], held.shape[1]
    rows, lanes = coeff_ref.shape[1], coeff_ref.shape[2]
    left = lax.broadcasted_iota(jnp.int32, (rows, lanes), 1) < lanes // 2
    tiles = []
    for half in range(2):
        one = coeff_ref[GROUP_ORDER.index(2 * half)].astype(F32)
        two = coeff_ref[GROUP_ORDER.index(2 * half + 1)].astype(F32)
        upper = jnp.where(left, one, pltpu.roll(two, lanes // 2, 1))
        lower = jnp.where(left, pltpu.roll(one, lanes // 2, 1), two)
        tiles.append(jnp.concatenate([upper, lower], axis=0).astype(BF16))
    coeff = jnp.concatenate(tiles, axis=1)
    coeff = jnp.concatenate([coeff, coeff], axis=0)
    copies = []
    for leaf in range(leaves):
        far = dot(far_ref[leaf * size : (leaf + 1) * size], coeff)
        held[leaf] = (near_ref[leaf] + far).astype(BF16)
        copy = pltpu.make_async_copy(held.at[leaf], out_ref.at[leaf], sems.at[leaf])
        copy.start()
        copies.append(copy)
    for copy in copies:
        copy.wait()


def call(kernel, outs, places, *args, to="v", scratch=(), name=None, flops=0, size=0):
    args = [pltpu.with_memory_space_constraint(a, pltpu.HBM) if p == "h" else a for p, a in zip(places, args, strict=True)]
    spaces = {"s": pltpu.SMEM, "v": pltpu.VMEM, "a": pl.ANY, "h": pltpu.HBM}
    return pl.pallas_call(
        kernel,
        out_shape=outs,
        in_specs=[pl.BlockSpec(memory_space=spaces[p]) for p in places],
        out_specs=jax.tree.map(lambda _: pl.BlockSpec(memory_space=spaces[to]), outs),
        scratch_shapes=scratch,
        compiler_params=pltpu.CompilerParams(vmem_limit_bytes=12 * 1024 * 1024),
        cost_estimate=pl.CostEstimate(flops=flops, bytes_accessed=size, transcendentals=0),
        name=name,
    )(*args)


def body(
    slip_rate,
    near_lists,
    near_blocks,
    source_basis,
    target_basis,
    leaf_up,
    leaf_down,
    strip_up,
    strip_down,
    strip_lists,
    coupling,
):
    along, dip, size, members = slip_rate.shape
    rank = source_basis.shape[2]
    leaves = along * dip
    n_row, n_col = lax.axis_size("row"), lax.axis_size("col")
    sds = jax.ShapeDtypeStruct
    slips = slip_rate.reshape(leaves, size, members)
    piece = (rank // 2, 128)

    dma = pltpu.SemaphoreType.DMA
    mega = 1024 * 1024
    basis = source_basis.reshape(leaves, rank, size)
    target = target_basis.reshape(leaves, rank, size)
    ups = leaf_up.reshape(leaves, rank, rank)
    downs = leaf_down.reshape(leaves, rank, rank)
    couplings = coupling[0]
    strips = couplings.shape[0]

    def room(value):
        return pltpu.VMEM(value.shape, value.dtype)

    parts = call(
        up_kernel,
        sds((n_col, *piece), BF16),
        "hhhh",
        strip_up[0],
        ups,
        basis,
        slips,
        scratch=[room(strip_up[0, :, 0]), room(ups), room(basis), room(slips), dma((strip_up.shape[1] + 3,))],
        name="up",
        flops=100_000_000,
        size=2 * mega,
    )
    up_row = [(i, i + 1) for i in range(n_row - 1)]
    down_row = [(j, i) for i, j in up_row]
    up_col = [(i, i + 1) for i in range(n_col - 1)]
    down_col = [(j, i) for i, j in up_col]

    edge = sds((dip, size, members), BF16)
    first, last = call(
        edges_kernel,
        (edge, edge),
        "va",
        slip_rate,
        parts,
        name="edges",
        flops=10_000_000_000,
        size=mega,
    )
    before = lax.ppermute(last, "row", up_row)
    after = lax.ppermute(first, "row", down_row)
    weights = call(
        weights_kernel,
        sds((4 * rank, n_row * rank // 2), BF16),
        "sva",
        strip_lists[0],
        couplings,
        first,
        scratch=[pltpu.VMEM((2 * rank, strips * rank // 2), F32)],
        name="weights",
        flops=100_000_000,
        size=mega,
    )
    parts = lax.all_to_all(parts, "col", 0, 0, tiled=True, axis_index_groups=[list(COL_ORDER)])
    tops = call(sum_kernel, sds((n_row, *piece), BF16), "va", parts, weights, name="sum", flops=30_000_000_000, size=mega // 2)
    rim_left, rim_right = call(
        rim_kernel,
        (sds((along + 2, size, members), BF16), sds((along + 2, size, members), BF16)),
        "vvva",
        slip_rate,
        before,
        after,
        tops,
        name="rim",
        flops=30_000_000_000,
        size=mega,
    )
    order = [(ROW_FIRST - i) % n_row for i in range(n_row)]
    tops = lax.all_to_all(tops, "row", 0, 0, tiled=True, axis_index_groups=[order])
    from_left = lax.ppermute(rim_right, "col", up_col)
    from_right = lax.ppermute(rim_left, "col", down_col)
    coeff = call(
        couple_kernel,
        sds((QUARTERS, *piece), BF16),
        "vv",
        tops,
        weights,
        name="couple",
        flops=30_000_000_000,
        size=mega // 2,
    )
    far = call(
        far_kernel,
        sds((leaves * size, 2 * rank), BF16),
        "vvva",
        strip_down[0],
        downs,
        target,
        coeff,
        name="far",
        flops=100_000_000,
        size=mega,
    )
    blocks = call(
        hold_kernel,
        sds(near_blocks.shape, BF16),
        "ha",
        near_blocks,
        coeff,
        scratch=[dma((1,))],
        name="hold",
        flops=1_000_000,
        size=2 * mega,
    )
    groups = [[i + at for at in GROUP_ORDER] for i in range(0, n_col, QUARTERS)]
    coeff = lax.all_to_all(coeff, "col", 0, 0, tiled=True, axis_index_groups=groups)
    near = call(
        near_kernel,
        sds((leaves, size, members), F32),
        "svvvvvv",
        near_lists.reshape(-1),
        slip_rate,
        before,
        after,
        from_left,
        from_right,
        blocks,
        scratch=[pltpu.VMEM(((along + 2) * (dip + 2), size, members), BF16)],
        name="near",
        flops=2 * leaves * 6 * size * size * members,
        size=4 * mega,
    )
    stress = call(
        final_kernel,
        sds((leaves, size, members), BF16),
        "vvv",
        near,
        far,
        coeff,
        to="a",
        scratch=[pltpu.VMEM((leaves, size, members), BF16), dma((leaves,))],
        name="final",
        flops=2 * leaves * size * members * rank * 2,
        size=2 * mega,
    )
    return stress.reshape(along, dip, size, members)


def solution(mesh):
    in_specs = (
        P("row", "col", None, None),
        P("row", "col", None),
        P("row", "col", None, None, None),
        P("row", "col", None, None),
        P("row", "col", None, None),
        P("row", "col", None, None),
        P("row", "col", None, None),
        P("row", None, None, None, None),
        P("row", None, None, None, None),
        P("row", None),
        P("row", None, None, None),
    )
    out_specs = P("row", "col", None, None)
    return jax.shard_map(body, mesh=mesh, in_specs=in_specs, out_specs=out_specs, check_vma=False)
```

```python
import jax
import jax.numpy as jnp
from jax import lax
from jax.experimental import pallas as pl
from jax.experimental.pallas import tpu as pltpu
from jax.sharding import PartitionSpec as P

F32 = jnp.float32
BF16 = jnp.bfloat16
QUARTERS = 4
COL_ORDER = (11, 0, 1, 2, 3, 4, 5, 6, 7, 15, 14, 13, 12, 10, 9, 8)
ROW_FIRST = 31


def halves(value):
    high = value.astype(BF16)
    return high, (value - high.astype(F32)).astype(BF16)


def dot(left, right):
    return jnp.dot(left, right, preferred_element_type=F32)


def dot_split(left, right):
    rows = left.shape[0]
    left_high, left_low = halves(left)
    right_high, right_low = halves(right)
    both = dot(jnp.concatenate([left_high, left_low], axis=0), right_high)
    return both[:rows] + both[rows:] + dot(left_high, right_low)


def chain_of(ref, col, levels):
    return [ref[level, (col >> level) & 1] for level in range(levels)]


def pack(tile, odd):
    half = tile.shape[0] // 2
    lane = lax.broadcasted_iota(jnp.int32, (half, tile.shape[1]), 1)
    left = lane < tile.shape[1] // 2
    upper, lower = tile[:half], tile[half:]
    shift = tile.shape[1] // 2
    if odd:
        return jnp.where(left, pltpu.roll(upper, shift, 1), lower)
    return jnp.where(left, upper, pltpu.roll(lower, shift, 1))


def fetch(refs, buffers, sems):
    copies = [
        pltpu.make_async_copy(ref, buffer, sems.at[at])
        for at, (ref, buffer) in enumerate(zip(refs, buffers, strict=True))
    ]
    for copy in copies:
        copy.start()
    return copies


def up_kernel(
    strip_up_ref, leaf_up_ref, basis_ref, slip_ref, out_ref, strip_up, leaf_up, basis, slip, sems
):
    leaves, levels = slip_ref.shape[0], strip_up.shape[0]
    col = lax.axis_index("col")
    copies = fetch(
        [strip_up_ref.at[level, (col >> level) & 1] for level in range(levels)]
        + [leaf_up_ref, basis_ref, slip_ref],
        [strip_up.at[level] for level in range(levels)] + [leaf_up, basis, slip],
        sems,
    )
    for copy in copies:
        copy.wait()
    chain = dot_split(dot_split(strip_up[3], strip_up[2]), dot_split(strip_up[1], strip_up[0]))
    ups = dot_split(chain, jnp.concatenate([leaf_up[leaf] for leaf in range(leaves)], axis=1))
    moments = jnp.concatenate([dot(basis[leaf], slip[leaf]) for leaf in range(leaves)], axis=0)
    node = dot_split(ups, moments)
    for quarter in range(QUARTERS):
        half = quarter // 2
        packed = pack(node[:, 128 * half : 128 * (half + 1)], quarter % 2).astype(BF16)
        for at, place in enumerate(COL_ORDER):
            if place % QUARTERS == quarter:
                out_ref[at] = packed


def sum_kernel(in_ref, after_ref, out_ref):
    del after_ref
    total = jnp.sum(in_ref[...].astype(F32), axis=0).astype(BF16)
    for copy in range(out_ref.shape[0]):
        out_ref[copy] = total


def weights_kernel(lists_ref, coupling_ref, after_ref, out_ref, wide):
    del after_ref
    strips, rank = coupling_ref.shape[0], coupling_ref.shape[1]
    half = rank // 2
    columns = out_ref.shape[1]
    row = lax.broadcasted_iota(jnp.int32, (half, columns), 0)
    column = lax.broadcasted_iota(jnp.int32, (half, columns), 1)
    chosen = []
    for strip in range(strips):
        place = (ROW_FIRST - lists_ref[strip]) & (columns // half - 1)
        chosen.append(jnp.where(column == row + place * half, 1.0, 0.0).astype(BF16))
    for strip in range(strips):
        at = slice(strip * half, (strip + 1) * half)
        wide[0:rank, at] = coupling_ref[strip, :, 0:half]
        wide[rank : 2 * rank, at] = coupling_ref[strip, :, half:rank]
    high, low = halves(wide[...])
    both = dot(jnp.concatenate([high, low], axis=0), jnp.concatenate(chosen, axis=0))
    out_ref[...] = both.astype(BF16)


def far_kernel(strip_down, leaf_down, target, after_ref, out_ref):
    del after_ref
    s0, s1, s2, s3 = chain_of(strip_down, lax.axis_index("col"), 4)
    chain = dot_split(dot_split(s0, s1), dot_split(s2, s3))
    leaves, rank, size = target.shape
    for leaf in range(leaves):
        down_high, down_low = halves(dot_split(leaf_down[leaf], chain))
        turned = target[leaf].astype(F32).T.astype(BF16)
        high, low = halves(dot(turned, down_high) + dot(turned, down_low))
        out_ref[leaf * size : (leaf + 1) * size, 0:rank] = high
        out_ref[leaf * size : (leaf + 1) * size, rank : 2 * rank] = low


def hold_kernel(blocks_ref, after_ref, out_ref, sems):
    del after_ref
    for copy in fetch((blocks_ref,), (out_ref,), sems):
        copy.wait()


def couple_kernel(tops_ref, weights_ref, out_ref):
    rank = weights_ref.shape[0] // 4
    half = rank // 2
    tops = tops_ref[...].reshape(tops_ref.shape[0] * tops_ref.shape[1], tops_ref.shape[2])
    product = dot(weights_ref[...], tops)
    product = product[: 2 * rank] + product[2 * rank :]
    upper, lower = product[:rank], product[rank:]
    lanes = product.shape[1]
    left = lax.broadcasted_iota(jnp.int32, (half, lanes), 1) < lanes // 2
    packed = jnp.where(
        left,
        upper[:half] + pltpu.roll(lower[:half], lanes // 2, 1),
        pltpu.roll(upper[half:], lanes // 2, 1) + lower[half:],
    ).astype(BF16)
    for copy in range(out_ref.shape[0]):
        out_ref[copy] = packed


def edges_kernel(slip_ref, after_ref, first_ref, last_ref):
    del after_ref
    first_ref[...] = slip_ref[0]
    last_ref[...] = slip_ref[slip_ref.shape[0] - 1]


def rim_kernel(slip_ref, before_ref, after_ref, after_sum_ref, left_ref, right_ref):
    del after_sum_ref
    along, dip = slip_ref.shape[0], slip_ref.shape[1]
    for ref, col in ((left_ref, 0), (right_ref, dip - 1)):
        ref[0] = before_ref[col]
        ref[along + 1] = after_ref[col]
        for row in range(along):
            ref[row + 1] = slip_ref[row, col]


def near_kernel(lists_ref, slip_ref, before_ref, after_ref, left_ref, right_ref, blocks_ref, out_ref, padded):
    along, dip, near = blocks_ref.shape[0], blocks_ref.shape[1], blocks_ref.shape[2]
    width = dip + 2
    for row in range(along + 2):
        padded[row * width] = left_ref[row]
        padded[row * width + width - 1] = right_ref[row]
    for col in range(dip):
        padded[1 + col] = before_ref[col]
        padded[(along + 1) * width + 1 + col] = after_ref[col]
        for row in range(along):
            padded[(row + 1) * width + 1 + col] = slip_ref[row, col]
    for row in range(along):
        for col in range(dip):
            leaf = row * dip + col
            sources = []
            for at in range(near):
                place = lists_ref[leaf * near + at]
                sources.append(padded[(row + place // 3) * width + col + place % 3])
            out_ref[leaf] = dot(
                jnp.concatenate([blocks_ref[row, col, at] for at in range(near)], axis=1),
                jnp.concatenate(sources, axis=0),
            )


def final_kernel(near_ref, far_ref, coeff_ref, out_ref, held, sems):
    leaves, size = held.shape[0], held.shape[1]
    rows, lanes = coeff_ref.shape[1], coeff_ref.shape[2]
    left = lax.broadcasted_iota(jnp.int32, (rows, lanes), 1) < lanes // 2
    tiles = []
    for half in range(2):
        one = coeff_ref[QUARTERS - 1 - 2 * half].astype(F32)
        two = coeff_ref[QUARTERS - 2 - 2 * half].astype(F32)
        upper = jnp.where(left, one, pltpu.roll(two, lanes // 2, 1))
        lower = jnp.where(left, pltpu.roll(one, lanes // 2, 1), two)
        tiles.append(jnp.concatenate([upper, lower], axis=0).astype(BF16))
    coeff = jnp.concatenate(tiles, axis=1)
    coeff = jnp.concatenate([coeff, coeff], axis=0)
    copies = []
    for leaf in range(leaves):
        far = dot(far_ref[leaf * size : (leaf + 1) * size], coeff)
        held[leaf] = (near_ref[leaf] + far).astype(BF16)
        copy = pltpu.make_async_copy(held.at[leaf], out_ref.at[leaf], sems.at[leaf])
        copy.start()
        copies.append(copy)
    for copy in copies:
        copy.wait()


def call(kernel, outs, places, *args, to="v", scratch=(), name=None, flops=0, size=0):
    args = [pltpu.with_memory_space_constraint(a, pltpu.HBM) if p == "h" else a for p, a in zip(places, args, strict=True)]
    spaces = {"s": pltpu.SMEM, "v": pltpu.VMEM, "a": pl.ANY, "h": pltpu.HBM}
    return pl.pallas_call(
        kernel,
        out_shape=outs,
        in_specs=[pl.BlockSpec(memory_space=spaces[p]) for p in places],
        out_specs=jax.tree.map(lambda _: pl.BlockSpec(memory_space=spaces[to]), outs),
        scratch_shapes=scratch,
        compiler_params=pltpu.CompilerParams(vmem_limit_bytes=12 * 1024 * 1024),
        cost_estimate=pl.CostEstimate(flops=flops, bytes_accessed=size, transcendentals=0),
        name=name,
    )(*args)


def body(
    slip_rate,
    near_lists,
    near_blocks,
    source_basis,
    target_basis,
    leaf_up,
    leaf_down,
    strip_up,
    strip_down,
    strip_lists,
    coupling,
):
    along, dip, size, members = slip_rate.shape
    rank = source_basis.shape[2]
    leaves = along * dip
    n_row, n_col = lax.axis_size("row"), lax.axis_size("col")
    sds = jax.ShapeDtypeStruct
    slips = slip_rate.reshape(leaves, size, members)
    piece = (rank // 2, 128)

    dma = pltpu.SemaphoreType.DMA
    mega = 1024 * 1024
    basis = source_basis.reshape(leaves, rank, size)
    target = target_basis.reshape(leaves, rank, size)
    ups = leaf_up.reshape(leaves, rank, rank)
    downs = leaf_down.reshape(leaves, rank, rank)
    couplings = coupling[0]
    strips = couplings.shape[0]

    def room(value):
        return pltpu.VMEM(value.shape, value.dtype)

    parts = call(
        up_kernel,
        sds((n_col, *piece), BF16),
        "hhhh",
        strip_up[0],
        ups,
        basis,
        slips,
        scratch=[room(strip_up[0, :, 0]), room(ups), room(basis), room(slips), dma((strip_up.shape[1] + 3,))],
        name="up",
        flops=100_000_000,
        size=2 * mega,
    )
    up_row = [(i, i + 1) for i in range(n_row - 1)]
    down_row = [(j, i) for i, j in up_row]
    up_col = [(i, i + 1) for i in range(n_col - 1)]
    down_col = [(j, i) for i, j in up_col]

    edge = sds((dip, size, members), BF16)
    first, last = call(
        edges_kernel,
        (edge, edge),
        "va",
        slip_rate,
        parts,
        name="edges",
        flops=10_000_000_000,
        size=mega,
    )
    before = lax.ppermute(last, "row", up_row)
    after = lax.ppermute(first, "row", down_row)
    weights = call(
        weights_kernel,
        sds((4 * rank, n_row * rank // 2), BF16),
        "sva",
        strip_lists[0],
        couplings,
        first,
        scratch=[pltpu.VMEM((2 * rank, strips * rank // 2), F32)],
        name="weights",
        flops=100_000_000,
        size=mega,
    )
    parts = lax.all_to_all(parts, "col", 0, 0, tiled=True, axis_index_groups=[list(COL_ORDER)])
    tops = call(sum_kernel, sds((n_row, *piece), BF16), "va", parts, weights, name="sum", flops=30_000_000_000, size=mega // 2)
    rim_left, rim_right = call(
        rim_kernel,
        (sds((along + 2, size, members), BF16), sds((along + 2, size, members), BF16)),
        "vvva",
        slip_rate,
        before,
        after,
        tops,
        name="rim",
        flops=30_000_000_000,
        size=mega,
    )
    order = [(ROW_FIRST - i) % n_row for i in range(n_row)]
    tops = lax.all_to_all(tops, "row", 0, 0, tiled=True, axis_index_groups=[order])
    from_left = lax.ppermute(rim_right, "col", up_col)
    from_right = lax.ppermute(rim_left, "col", down_col)
    coeff = call(
        couple_kernel,
        sds((QUARTERS, *piece), BF16),
        "vv",
        tops,
        weights,
        name="couple",
        flops=30_000_000_000,
        size=mega // 2,
    )
    far = call(
        far_kernel,
        sds((leaves * size, 2 * rank), BF16),
        "vvva",
        strip_down[0],
        downs,
        target,
        coeff,
        name="far",
        flops=100_000_000,
        size=mega,
    )
    blocks = call(
        hold_kernel,
        sds(near_blocks.shape, BF16),
        "ha",
        near_blocks,
        coeff,
        scratch=[dma((1,))],
        name="hold",
        flops=1_000_000,
        size=2 * mega,
    )
    groups = [list(range(i, i + QUARTERS))[::-1] for i in range(0, n_col, QUARTERS)]
    coeff = lax.all_to_all(coeff, "col", 0, 0, tiled=True, axis_index_groups=groups)
    near = call(
        near_kernel,
        sds((leaves, size, members), F32),
        "svvvvvv",
        near_lists.reshape(-1),
        slip_rate,
        before,
        after,
        from_left,
        from_right,
        blocks,
        scratch=[pltpu.VMEM(((along + 2) * (dip + 2), size, members), BF16)],
        name="near",
        flops=2 * leaves * 6 * size * size * members,
        size=4 * mega,
    )
    stress = call(
        final_kernel,
        sds((leaves, size, members), BF16),
        "vvv",
        near,
        far,
        coeff,
        to="a",
        scratch=[pltpu.VMEM((leaves, size, members), BF16), dma((leaves,))],
        name="final",
        flops=2 * leaves * size * members * rank * 2,
        size=2 * mega,
    )
    return stress.reshape(along, dip, size, members)


def solution(mesh):
    in_specs = (
        P("row", "col", None, None),
        P("row", "col", None),
        P("row", "col", None, None, None),
        P("row", "col", None, None),
        P("row", "col", None, None),
        P("row", "col", None, None),
        P("row", "col", None, None),
        P("row", None, None, None, None),
        P("row", None, None, None, None),
        P("row", None),
        P("row", None, None, None),
    )
    out_specs = P("row", "col", None, None)
    return jax.shard_map(body, mesh=mesh, in_specs=in_specs, out_specs=out_specs, check_vma=False)
```
